256 devices in a mesh: ia: 8 (over x_hi, y), ja: 4 (over x_lo, core), vert: 8 (over z).
Axes of the slice: x: 4 (x_hi: 2, x_lo: 2; x = x_hi * 2 + x_lo), y: 4, z: 8, core: 2. Of those that a mesh axis runs over, the one named last changes fastest.
Arguments:
- amplitudes: bfloat16 [80, 80, 4096], P('ia', 'ja', 'vert'), may hold values from -6 to 6
- ladder_w: bfloat16 [80, 80, 6400], P('ia', 'ja'), may hold values from -0.078125 to 0.078125
- ph_left: bfloat16 [80, 512, 5120], P('ia', 'vert'), may hold values from -6 to 6
- ph_right: bfloat16 [80, 512, 5120], P('ia', 'vert', 'ja'), may hold values from -0.03125 to 0.03125
- occ_sym: int32 [80], replicated, may hold values from 0 to 7
- vir_sym: int32 [64], replicated, may hold values from 0 to 7
Outputs:
- residual: bfloat16 [80, 80, 4096], P('ia', 'ja', 'vert')
The draws below stay inside these ranges and needn't reach their ends.
Inputs may be any that keep to these rules, and one draw needn't show every extreme that they name: `occ_sym`: D2h irrep labels, combined by bitwise xor. `vir_sym`: D2h irrep labels, combined by bitwise xor.
All inputs are finite; a program needn't handle non-finite values.
Results may differ from the reference program's by a relative error of at most 0.001.
Values may be sent and summed in bfloat16 or wider, within the bound.
No kernel may reach another device: no remote copies, remote signals or barrier semaphores. Data moves between devices by JAX's collectives and lax.ppermute only.
A program may use at most 192 MiB of HBM per device.

```python
import jax
import jax.numpy as jnp

O = 80
SLAB = 64
NC = 512
PAIRS = 4096


def plant(entries, stream_key, low, top_value):
    place = [jax.random.randint(jax.random.fold_in(stream_key, axis), (), 0, length) for axis, length in enumerate(entries.shape)]
    main_axis = entries.shape.index(max(entries.shape))
    next_to = place[:main_axis] + [(place[main_axis] + 1) % entries.shape[main_axis]] + place[main_axis + 1:]
    return entries.at[tuple(place)].set(low).at[tuple(next_to)].set(top_value)


def steps_of(stream_key, dims, split, least, largest):
    loudness = 1.0
    for dim, parts in split:
        heights = jax.random.uniform(jax.random.fold_in(jax.random.fold_in(stream_key, 6), dim), (parts,), jnp.float32, least / len(split), largest / len(split))
        loudness = loudness * jnp.repeat(jnp.exp(heights), dims[dim] // parts).reshape((-1,) + (1,) * (len(dims) - 1 - dim))
    return loudness


def scatter_about(stream_key, dims, scale, bound, cuts=(), kind=jnp.bfloat16):
    array = scale * jax.random.normal(stream_key, dims, jnp.float32)
    if cuts:
        array = array * steps_of(stream_key, dims, cuts, -0.22, 0.18)
    return jnp.clip(array, -bound, bound).astype(kind)


def setup_inputs(seed: int = 0) -> dict:
    seeds = jax.random.split(jax.random.key(seed), 7)
    amplitudes = scatter_about(seeds[0], (O, O, PAIRS), 1.0, 6.0, ((0, 8), (1, 4), (2, 8)))
    ladder_w = scatter_about(seeds[1], (O, O, O * O), (O * O) ** -0.5, 0.078125, ((0, 8), (1, 4)))
    ph_left = scatter_about(seeds[2], (O, NC, O * SLAB), 1.0, 6.0, ((0, 8), (1, 8)))
    ph_right = scatter_about(seeds[3], (O, NC, O * SLAB), (O * NC) ** -0.5, 0.03125, ((0, 8), (1, 8), (2, 4)))
    occ_sym = plant(jax.random.randint(seeds[4], (O,), 0, 8), jax.random.fold_in(seeds[4], 1), 0, 7).astype(jnp.int32)
    vir_sym = plant(jax.random.randint(seeds[5], (SLAB,), 0, 8), jax.random.fold_in(seeds[5], 1), 0, 7).astype(jnp.int32)
    return dict(amplitudes=amplitudes, ladder_w=ladder_w, ph_left=ph_left, ph_right=ph_right, occ_sym=occ_sym, vir_sym=vir_sym)


def reference(amplitudes, ladder_w, ph_left, ph_right, occ_sym, vir_sym):
    left = ph_left.astype(jnp.float32).reshape(O, NC, O, SLAB)
    right = ph_right.astype(jnp.float32).reshape(O, NC, O, SLAB)
    phterm = jnp.einsum("icka,kcjb->ijab", left, right)
    anti = phterm - jnp.swapaxes(phterm, 2, 3)
    anti = anti.reshape(O, O, SLAB * SLAB)
    weights = ladder_w.astype(jnp.float32).reshape(O, O, O, O)
    ladder = jnp.einsum("ijkl,klp->ijp", weights, amplitudes.astype(jnp.float32))
    sym_ij = jnp.bitwise_xor(occ_sym[:, None], occ_sym[None, :])
    sym_ab = jnp.bitwise_xor(vir_sym[:, None], vir_sym[None, :]).reshape(SLAB * SLAB)
    mask = (jnp.bitwise_xor(sym_ij[:, :, None], sym_ab[None, None, :]) == 0).astype(jnp.float32)
    return (mask * (anti + ladder)).astype(jnp.bfloat16)
```

```python
import functools

import jax
import jax.numpy as jnp
from jax import lax
from jax.experimental import pallas as pl
from jax.experimental.pallas import tpu as pltpu
from jax.sharding import PartitionSpec as P

F32 = jnp.float32
BF16 = jnp.bfloat16
SCALE = 32.0
CHUNKS = (10, 10)


def swap_blocks(tile):
    turned = tile.T
    top, bottom = turned[:64], turned[64:]
    low = lax.broadcasted_iota(jnp.int32, (64, 128), 1) < 64
    return (
        jnp.where(low, top, pltpu.roll(bottom, 64, 1)),
        jnp.where(low, pltpu.roll(top, 64, 1), bottom),
    )


def turn_body(index, u, out):
    pairs_i, pairs_k = u.shape[0] // 2, u.shape[2] // 128

    def step(ip, carry):
        for kp in range(pairs_k):
            lanes = slice(128 * kp, 128 * kp + 128)
            tile = jnp.concatenate([u[2 * ip, :, lanes], u[2 * ip + 1, :, lanes]], axis=0)
            first, second = swap_blocks(tile.astype(F32))
            row = pl.multiple_of(ip * 128, 128)
            out[0, pl.ds(row, 64), lanes] = first.astype(BF16)
            out[0, pl.ds(row + 64, 64), lanes] = second.astype(BF16)
        return carry

    lax.fori_loop(0, pairs_i, step, 0)


def turn_slabs(u, index):
    count, size = index.shape[0], u.shape[0] * 64
    return pl.pallas_call(
        turn_body,
        out_shape=jax.ShapeDtypeStruct((count, size, size), BF16),
        grid_spec=pltpu.PrefetchScalarGridSpec(
            num_scalar_prefetch=1,
            grid=(count,),
            in_specs=[pl.BlockSpec((u.shape[0], 64, size), lambda s, index: (0, 0, index[s]))],
            out_specs=pl.BlockSpec((1, size, size), lambda s, index: (s, 0, 0)),
        ),
        compiler_params=pltpu.CompilerParams(vmem_limit_bytes=40 << 20),
        cost_estimate=pl.CostEstimate(flops=0, bytes_accessed=count * 1638400 * 4, transcendentals=0),
    )(index.astype(jnp.int32), u)


def product_body(place, u, v0, v1, v2a, v2b, v3, out, total):
    shift, z = place[0], place[1]
    width = out.shape[2]
    parts = [v0[...], v1[...], jnp.concatenate([v2a[...], v2b[...]], axis=0), v3[...]]
    dots = [
        jnp.dot(u[lax.rem(shift + d, 4)], parts[d], preferred_element_type=F32) for d in range(4)
    ]
    total[...] = functools.reduce(lambda p, q: p + q, dots)

    def step(ip, carry):
        row = pl.multiple_of(ip * 128, 128)
        for jp in range(width // 128):
            lanes = slice(128 * jp, 128 * jp + 128)
            tile = total[pl.ds(row, 128), lanes]
            first, second = swap_blocks(tile)
            total[pl.ds(row, 64), lanes] = tile[:64] - first
            total[pl.ds(row + 64, 64), lanes] = tile[64:] - second
            for d in range(8):
                a = pl.multiple_of(lax.rem(z + d, 8) * 8, 8)
                out[d, pl.ds(pl.multiple_of(16 * ip, 16), 8), lanes] = total[pl.ds(row + a, 8), lanes]
                out[d, pl.ds(pl.multiple_of(16 * ip + 8, 8), 8), lanes] = total[
                    pl.ds(row + 64 + a, 8), lanes
                ]
        return carry

    lax.fori_loop(0, total.shape[0] // 128, step, 0)


def product(place, u, parts):
    size, width = u.shape[1], parts[0].shape[1]
    whole = lambda x: pl.BlockSpec(x.shape, lambda s, place: (0,) * x.ndim)
    out = jax.ShapeDtypeStruct((8, size // 8, width), F32)
    return pl.pallas_call(
        product_body,
        out_shape=out,
        grid_spec=pltpu.PrefetchScalarGridSpec(
            num_scalar_prefetch=1,
            grid=(1,),
            in_specs=[whole(u)] + [whole(p) for p in parts],
            out_specs=whole(out),
            scratch_shapes=[pltpu.VMEM((size, width), F32)],
        ),
        compiler_params=pltpu.CompilerParams(vmem_limit_bytes=40 << 20),
        cost_estimate=pl.CostEstimate(
            flops=2 * size * 4 * size * width * 3, bytes_accessed=8 << 20, transcendentals=0
        ),
    )(place.astype(jnp.int32), u, *parts)


def ring(n, shift):
    return [(i, (i + shift) % n) for i in range(n)]


def y_ring(shift):
    return [(4 * h + y, 4 * h + (y + shift) % 4) for h in range(2) for y in range(4)]


X_HI = [(i, (i + 4) % 8) for i in range(8)]
CORE = [(j, j ^ 1) for j in range(4)]
X_LO = [(j, j ^ 2) for j in range(4)]
X_CROSS = [(4 * i + j, 4 * ((i + 4) % 8) + (j ^ 2)) for i in range(8) for j in range(4)]


def after(value, *others):
    return lax.optimization_barrier((value,) + others)[0]


def sort_body(w, order, out):
    out[...] = jnp.dot(w[...], order[...], preferred_element_type=F32).astype(BF16)


def sort_columns(weights, occ, cols_j):
    rows, width = weights.shape[0], 8 * occ
    column = jnp.arange(width)
    block, rest = column // (8 * cols_j), column % (8 * cols_j)
    source = (rest // cols_j) * occ + block * cols_j + rest % cols_j
    order = (jnp.arange(width)[:, None] == source[None, :]).astype(BF16)
    return pl.pallas_call(
        sort_body,
        out_shape=jax.ShapeDtypeStruct(weights.shape, BF16),
        grid=(weights.shape[1] // width,),
        in_specs=[
            pl.BlockSpec((rows, width), lambda s: (0, s)),
            pl.BlockSpec((width, width), lambda s: (0, 0)),
        ],
        out_specs=pl.BlockSpec((rows, width), lambda s: (0, s)),
        compiler_params=pltpu.CompilerParams(vmem_limit_bytes=24 << 20),
        cost_estimate=pl.CostEstimate(
            flops=2 * rows * weights.shape[1] * width, bytes_accessed=6 << 20, transcendentals=0
        ),
    )(weights, order)


def ladder_body(place, w, near, far, out, full):
    run = near.shape[1] // 5
    for half in range(2):
        for block in range(4):
            x = (half ^ place[0]) * 2 + ((block // 2) ^ place[1])
            for group in range(5):
                to = slice((half * 20 + group * 4 + block) * run, (half * 20 + group * 4 + block + 1) * run)
                rows = slice(group * run, group * run + run)

                @pl.when(block % 2 == place[2])
                def _():
                    full[to, :] = near[x, rows, :]

                @pl.when(block % 2 != place[2])
                def _():
                    full[to, :] = far[x, rows, :]

    out[...] = jnp.dot(w[...], full[...], preferred_element_type=F32)


def ladder_sum(place, weights, near, far):
    whole = lambda x: pl.BlockSpec(x.shape, lambda s, place: (0,) * x.ndim)
    out = jax.ShapeDtypeStruct((weights.shape[0], near.shape[2]), F32)
    return pl.pallas_call(
        ladder_body,
        out_shape=out,
        grid_spec=pltpu.PrefetchScalarGridSpec(
            num_scalar_prefetch=1,
            grid=(1,),
            in_specs=[whole(weights), whole(near), whole(far)],
            out_specs=whole(out),
            scratch_shapes=[pltpu.VMEM((weights.shape[1], near.shape[2]), BF16)],
        ),
        compiler_params=pltpu.CompilerParams(vmem_limit_bytes=40 << 20),
        cost_estimate=pl.CostEstimate(
            flops=2 * weights.shape[0] * weights.shape[1] * near.shape[2] * 2,
            bytes_accessed=10 << 20,
            transcendentals=0,
        ),
    )(place.astype(jnp.int32), weights, near, far)


def body(amplitudes, ladder_w, ph_left, ph_right, occ_sym, vir_sym):
    rows_i, local_c = ph_left.shape[:2]
    slab = vir_sym.shape[0]
    occ = occ_sym.shape[0]
    cols_j = ph_right.shape[2] // slab
    rows_a = slab // 8
    ia, ja, z = lax.axis_index("ia"), lax.axis_index("ja"), lax.axis_index("vert")
    h, y, core = ia // 4, ia % 4, ja % 2
    around = (y + jnp.arange(4)) % 4

    mine = turn_slabs(ph_left, (1 - h) * 4 + jnp.roll(around, -2 * core)[:2])
    got = lax.ppermute(mine, ("ia", "ja"), X_CROSS)
    got_core = lax.ppermute(got, "ja", CORE)
    left = turn_slabs(ph_left, h * 4 + around)
    other = jnp.concatenate([got, got_core], axis=0)

    right = ph_right.reshape(rows_i * local_c, cols_j * slab)
    half = rows_i * local_c // 2
    pieces, start = [], 0
    up = down = None
    for count in CHUNKS:
        v0 = lax.slice_in_dim(right, start * slab, (start + count) * slab, axis=1)
        start += count
        sent = v0 if up is None else after(v0, up, down)
        up = lax.ppermute(sent, "ia", y_ring(1))
        down = lax.ppermute(sent, "ia", y_ring(-1))
        v2a = lax.ppermute(up[:half], "ia", y_ring(1))
        v2b = lax.ppermute(down[half:], "ia", y_ring(-1))
        pieces.append((v0, down, v2a, v2b, up))

    t = amplitudes.reshape(rows_i * cols_j, amplitudes.shape[2])
    t = after(t, pieces[0][1], pieces[0][4])
    ty = [t] + [lax.ppermute(t, "ia", y_ring(-d)) for d in (1, 2, 3)]
    ty = lax.dynamic_slice_in_dim(jnp.stack(ty + ty), (4 - y) % 4, 4, 0)
    ty = after(ty, got).reshape(4 * rows_i * cols_j, -1)
    tx = [ty, lax.ppermute(ty, "ja", X_LO), lax.ppermute(ty, "ia", X_HI)]
    tx.append(lax.ppermute(ty, ("ia", "ja"), X_CROSS))
    near = jnp.stack(tx)
    far = lax.ppermute(near, "ja", CORE)

    sums = []
    for parts in pieces:
        theirs = product(jnp.stack([2 * core, z]), other, parts)
        ours = product(jnp.stack([jnp.zeros_like(z), z]), left, parts)
        theirs = lax.ppermute((theirs * SCALE).astype(jnp.float16), "ia", X_HI)
        sent = [ours[d] + theirs[d].astype(F32) * (1.0 / SCALE) for d in range(8)]
        arrived = [
            lax.ppermute((sent[d] * SCALE).astype(jnp.float16), "vert", ring(8, d)).astype(F32)
            for d in range(1, 8)
        ]
        sums.append(sent[0] + functools.reduce(lambda p, q: p + q, arrived) * (1.0 / SCALE))
    anti = jnp.concatenate(sums, axis=1).reshape(rows_i, rows_a, cols_j, slab)
    anti = anti.transpose(0, 2, 1, 3).reshape(rows_i, cols_j, rows_a * slab)

    weights = sort_columns(ladder_w.reshape(rows_i * cols_j, occ * occ), occ, cols_j)
    ladder = ladder_sum(jnp.stack([h, ja // 2, core]), weights, near, far).reshape(anti.shape)

    sym_i = lax.dynamic_slice_in_dim(occ_sym, ia * rows_i, rows_i, 0)
    sym_j = lax.dynamic_slice_in_dim(occ_sym, ja * cols_j, cols_j, 0)
    sym_a = lax.dynamic_slice_in_dim(vir_sym, z * rows_a, rows_a, 0)
    sym_ij = jnp.bitwise_xor(sym_i[:, None], sym_j[None, :])
    sym_ab = jnp.bitwise_xor(sym_a[:, None], vir_sym[None, :]).reshape(rows_a * slab)
    mask = (jnp.bitwise_xor(sym_ij[:, :, None], sym_ab[None, None, :]) == 0).astype(F32)
    return (mask * (anti + ladder)).astype(BF16)


def solution(mesh):
    in_specs = (
        P("ia", "ja", "vert"),
        P("ia", "ja", None),
        P("ia", "vert", None),
        P("ia", "vert", "ja"),
        P(),
        P(),
    )
    out_specs = P("ia", "ja", "vert")
    return jax.shard_map(body, mesh=mesh, in_specs=in_specs, out_specs=out_specs, check_vma=False)
```

```python
import functools

import jax
import jax.numpy as jnp
from jax import lax
from jax.experimental import pallas as pl
from jax.experimental.pallas import tpu as pltpu
from jax.sharding import PartitionSpec as P

F32 = jnp.float32
BF16 = jnp.bfloat16
SCALE = 32.0
FIRST = 10


def cost(us):
    return pl.CostEstimate(flops=int(us * 1e9), bytes_accessed=int(us * 3e6), transcendentals=0)


def swap_blocks(tile):
    turned = tile.T
    top, bottom = turned[:64], turned[64:]
    low = lax.broadcasted_iota(jnp.int32, (64, 128), 1) < 64
    return (
        jnp.where(low, top, pltpu.roll(bottom, 64, 1)),
        jnp.where(low, pltpu.roll(top, 64, 1), bottom),
    )


def turn_body(index, u, out):
    for ip in range(u.shape[0] // 2):
        for kp in range(u.shape[2] // 128):
            lanes = slice(128 * kp, 128 * kp + 128)
            tile = jnp.concatenate([u[2 * ip, :, lanes], u[2 * ip + 1, :, lanes]], axis=0)
            first, second = swap_blocks(tile)
            out[128 * ip : 128 * ip + 64, lanes] = first
            out[128 * ip + 64 : 128 * ip + 128, lanes] = second


def turn_slabs(u, index):
    count, size = index.shape[0], u.shape[0] * 64
    return pl.pallas_call(
        turn_body,
        out_shape=jax.ShapeDtypeStruct((size, count * size), BF16),
        grid_spec=pltpu.PrefetchScalarGridSpec(
            num_scalar_prefetch=1,
            grid=(count,),
            in_specs=[pl.BlockSpec((u.shape[0], 64, size), lambda s, index: (0, 0, index[s]))],
            out_specs=pl.BlockSpec((size, size), lambda s, index: (0, s)),
        ),
        compiler_params=pltpu.CompilerParams(vmem_limit_bytes=60 << 20),
        cost_estimate=cost(0.5 * count),
    )(index.astype(jnp.int32), u)


def near_body(place, near, far, v0, v1, v3, out, left, right):
    size = near.shape[0]

    @pl.when(place[0] == 0)
    def _():
        left[...] = near[:, :size]
        right[:size, :] = v1[...]
        right[size : 2 * size, :] = v3[...]

    @pl.when(place[0] != 0)
    def _():
        left[...] = far[:, :size]
        right[:size, :] = v3[...]
        right[size : 2 * size, :] = v1[...]

    for low, high in ((0, 384), (384, 640)):
        total = jnp.dot(near[low:high, size:], right[:size, :], preferred_element_type=F32)
        total += jnp.dot(far[low:high, size:], right[size:, :], preferred_element_type=F32)
        out[low:high, :] = total + jnp.dot(left[low:high, :], v0[...], preferred_element_type=F32)


def product_near(place, left, parts):
    size, width = parts[0].shape
    side = lambda at: pl.BlockSpec((size, 2 * size), lambda s, place: (0, at))
    whole = lambda x: pl.BlockSpec(x.shape, lambda s, place: (0,) * x.ndim)
    out = jax.ShapeDtypeStruct((size, width), F32)
    return pl.pallas_call(
        near_body,
        out_shape=out,
        grid_spec=pltpu.PrefetchScalarGridSpec(
            num_scalar_prefetch=1,
            grid=(1,),
            in_specs=[side(0), side(2 - len(left))] + [whole(x) for x in parts],
            out_specs=whole(out),
            scratch_shapes=[pltpu.VMEM((size, size), BF16), pltpu.VMEM((2 * size, width), BF16)],
        ),
        compiler_params=pltpu.CompilerParams(vmem_limit_bytes=32 << 20),
        cost_estimate=cost(1),
    )(place.astype(jnp.int32).reshape(1), left[0], left[-1], *parts)


def product_body(start, place, partial_sum, near, far, v2a, v2b, out, left):
    size, width = near.shape[0], out.shape[2]
    columns = slice(start, start + width)

    @pl.when(place[0] == 0)
    def _():
        left[...] = far[...]

    @pl.when(place[0] != 0)
    def _():
        left[...] = near[...]

    right = jnp.concatenate([v2a[:, columns], v2b[:, columns]], axis=0)
    for low, high in ((0, 384), (384, 640)):
        total = partial_sum[low:high, columns]
        total += jnp.dot(left[low:high, :], right, preferred_element_type=F32)
        for at in range(low, high, 128):
            for jp in range(width // 128):
                lanes = slice(128 * jp, 128 * jp + 128)
                tile = total[at - low : at - low + 128, lanes]
                first, second = swap_blocks(tile)
                first, second = tile[:64] - first, tile[64:] - second
                for z in range(8):
                    out[z, at // 8 : at // 8 + 8, lanes] = first[8 * z : 8 * z + 8]
                    out[z, at // 8 + 8 : at // 8 + 16, lanes] = second[8 * z : 8 * z + 8]


def product(place, left, partial_sum, parts, start, width):
    size = partial_sum.shape[0]
    side = lambda at: pl.BlockSpec((size, size), lambda s, place: (0, at))
    whole = lambda x: pl.BlockSpec(x.shape, lambda s, place: (0,) * x.ndim)
    out = jax.ShapeDtypeStruct((8, size // 8, width), F32)
    return pl.pallas_call(
        functools.partial(product_body, start),
        out_shape=out,
        grid_spec=pltpu.PrefetchScalarGridSpec(
            num_scalar_prefetch=1,
            grid=(1,),
            in_specs=[whole(partial_sum), side(0), side(2 * (2 - len(left)))]
            + [whole(x) for x in parts],
            out_specs=whole(out),
            scratch_shapes=[pltpu.VMEM((size, size), BF16)],
        ),
        compiler_params=pltpu.CompilerParams(vmem_limit_bytes=24 << 20),
        cost_estimate=cost(1),
    )(place.astype(jnp.int32).reshape(1), partial_sum, left[0], left[-1], *parts)


def ring(n, shift):
    return [(i, (i + shift) % n) for i in range(n)]


def y_ring(shift):
    return [(4 * h + y, 4 * h + (y + shift) % 4) for h in range(2) for y in range(4)]


X_HI = [(i, (i + 4) % 8) for i in range(8)]
CORE = [(j, j ^ 1) for j in range(4)]
X_LO = [(j, j ^ 2) for j in range(4)]
X_CROSS = [(4 * i + j, 4 * ((i + 4) % 8) + (j ^ 2)) for i in range(8) for j in range(4)]


def after(*values):
    return lax.optimization_barrier(values)


def sort_body(w, order, out, rows):
    count = w.shape[1]
    for i in range(w.shape[0]):
        rows[count * i : count * i + count, :] = w[i].astype(F32)
    out[...] = jnp.dot(rows[...].astype(BF16), order[...], preferred_element_type=F32).astype(BF16)


def sort_columns(weights, order):
    rows_i, cols_j, columns = weights.shape
    rows, width = rows_i * cols_j, order.shape[0]
    return pl.pallas_call(
        sort_body,
        out_shape=jax.ShapeDtypeStruct((rows, columns), BF16),
        grid=(columns // width,),
        in_specs=[
            pl.BlockSpec((rows_i, cols_j, width), lambda s: (0, 0, s)),
            pl.BlockSpec((width, width), lambda s: (0, 0)),
        ],
        out_specs=pl.BlockSpec((rows, width), lambda s: (0, s)),
        scratch_shapes=[pltpu.VMEM((rows, width), F32)],
        compiler_params=pltpu.CompilerParams(vmem_limit_bytes=24 << 20),
        cost_estimate=cost(1),
    )(weights, order)


def arrival_order(occ, cols_j):
    width = 8 * occ
    column = jnp.arange(width)
    block, rest = column // (8 * cols_j), column % (8 * cols_j)
    source = (rest // cols_j) * occ + block * cols_j + rest % cols_j
    return (jnp.arange(width)[:, None] == source[None, :]).astype(BF16)


def order_body(start, own, down, two_a, two_b, up, out):
    count = own.shape[0]
    for n in range(count):
        for d, part in ((0, own), (1, down), (3, up)):
            out[n, lax.rem(start[0] + d, 4)] = part[n]
        two = (two_a, two_b)[n // (count // 2)]
        out[n, lax.rem(start[0] + 2, 4)] = two[n % (count // 2)]


def order_pieces(start, pieces):
    whole = lambda x: pl.BlockSpec(x.shape, lambda s, start: (0,) * x.ndim)
    count, rows, width = pieces[0].shape
    out = jax.ShapeDtypeStruct((count, 4, rows, width), BF16)
    return pl.pallas_call(
        order_body,
        out_shape=out,
        grid_spec=pltpu.PrefetchScalarGridSpec(
            num_scalar_prefetch=1,
            grid=(1,),
            in_specs=[whole(x) for x in pieces],
            out_specs=whole(out),
        ),
        compiler_params=pltpu.CompilerParams(vmem_limit_bytes=16 << 20),
        cost_estimate=cost(0.5),
    )(start.astype(jnp.int32).reshape(1), *pieces).reshape(count, 4 * rows, width)


def ladder_body(place, w, near, far, out, full):
    run = near.shape[1] // 5
    for half in range(2):
        for block in range(4):
            x = (half ^ place[0]) * 2 + ((block // 2) ^ place[1])
            for group in range(5):
                at = (half * 20 + group * 4 + block) * run
                rows = slice(group * run, group * run + run)

                @pl.when(block % 2 == place[2])
                def _():
                    full[at : at + run, :] = near[x, rows, :]

                @pl.when(block % 2 != place[2])
                def _():
                    full[at : at + run, :] = far[x, rows, :]

    rows = out.shape[1]
    total = jnp.dot(w[...], full[...], preferred_element_type=F32)
    for i in range(out.shape[0]):
        out[i] = total[rows * i : rows * i + rows]


def ladder_sum(place, weights, near, far, rows_i):
    whole = lambda x: pl.BlockSpec(x.shape, lambda s, place: (0,) * x.ndim)
    out = jax.ShapeDtypeStruct((rows_i, weights.shape[0] // rows_i, near.shape[2]), F32)
    return pl.pallas_call(
        ladder_body,
        out_shape=out,
        grid_spec=pltpu.PrefetchScalarGridSpec(
            num_scalar_prefetch=1,
            grid=(1,),
            in_specs=[whole(weights), whole(near), whole(far)],
            out_specs=whole(out),
            scratch_shapes=[pltpu.VMEM((weights.shape[1], near.shape[2]), BF16)],
        ),
        compiler_params=pltpu.CompilerParams(vmem_limit_bytes=28 << 20),
        cost_estimate=cost(1),
    )(place.astype(jnp.int32), weights, near, far)


def finish_body(sym_i, sum0, own0, sum1, own1, ladder, table, out, rows):
    low = lax.broadcasted_iota(jnp.int32, (8, 128), 1) < 64
    for i in range(out.shape[0]):
        j = 0
        for part, own in ((sum0, own0), (sum1, own1)):
            for jp in range(part.shape[1] // 128):
                at = slice(8 * i, 8 * i + 8), slice(128 * jp, 128 * jp + 128)
                tile = (part[at] + own[at]) * (1.0 / SCALE)
                turned = pltpu.roll(tile, 64, 1)
                even = jnp.where(low, tile, pltpu.roll(turned, 7, 0))
                odd = jnp.where(low, turned, pltpu.roll(tile, 7, 0))
                for ap in range(4):
                    rows[i, ap, j : j + 1, :] = even[2 * ap : 2 * ap + 1]
                    rows[i, ap, j + 1 : j + 2, :] = odd[2 * ap : 2 * ap + 1]
                j += 2
        for ap in range(4):
            lanes = slice(128 * ap, 128 * ap + 128)
            value = rows[i, ap] + ladder[i, :, lanes]
            out[i, :, lanes] = jnp.where(table[:, lanes] == sym_i[i], value, 0.0).astype(BF16)


def finish(sym_i, sums, ladder, table):
    whole = lambda x: pl.BlockSpec(x.shape, lambda s, sym_i: (0,) * x.ndim)
    rows_i, cols_j, width = ladder.shape
    return pl.pallas_call(
        finish_body,
        out_shape=jax.ShapeDtypeStruct(ladder.shape, BF16),
        grid_spec=pltpu.PrefetchScalarGridSpec(
            num_scalar_prefetch=1,
            grid=(1,),
            in_specs=[whole(x) for x in (*sums, ladder, table)],
            out_specs=whole(ladder),
            scratch_shapes=[pltpu.VMEM((rows_i, width // 128, cols_j, 128), F32)],
        ),
        compiler_params=pltpu.CompilerParams(vmem_limit_bytes=56 << 20),
        cost_estimate=cost(1),
    )(sym_i, *sums, ladder, table)


def body(amplitudes, ladder_w, ph_left, ph_right, occ_sym, vir_sym):
    rows_i, local_c = ph_left.shape[:2]
    slab = vir_sym.shape[0]
    occ = occ_sym.shape[0]
    cols_j = ph_right.shape[2] // slab
    rows_a = slab // 8
    ia, ja, z = lax.axis_index("ia"), lax.axis_index("ja"), lax.axis_index("vert")
    h, y, core = ia // 4, ia % 4, ja % 2
    around = (y + jnp.arange(4)) % 4

    right = ph_right.reshape(rows_i * local_c, cols_j * slab)
    half = rows_i * local_c // 2
    up = lax.ppermute(right, "ia", y_ring(1))
    down = lax.ppermute(right, "ia", y_ring(-1))
    t = amplitudes.reshape(rows_i * cols_j, -1)
    tx = [t, lax.ppermute(t, "ja", X_LO), lax.ppermute(t, "ia", X_HI)]
    tx.append(lax.ppermute(t, ("ia", "ja"), X_CROSS))
    mine = turn_slabs(ph_left, (1 - h) * 4 + jnp.roll(around, -2 * core)[:2])
    got = lax.ppermute(mine, ("ia", "ja"), X_CROSS)
    ph_left, mine = after(ph_left, mine)
    left = turn_slabs(ph_left, h * 4 + around)
    w, left, order = after(ladder_w, left, arrival_order(occ, cols_j))
    weights = sort_columns(w, order)

    up, down, weights = after(up, down, weights)
    v2a = lax.ppermute(up[:half], "ia", y_ring(1))
    v2b = lax.ppermute(down[half:], "ia", y_ring(-1))
    flat = jnp.zeros_like(z)
    ours = product_near(flat, (left,), (right, down, up))
    got, ours = after(got, ours)
    got_core = lax.ppermute(got, "ja", CORE)
    theirs = product_near(core, (got, got_core), (right, down, up))

    theirs, ours, *tx = after(theirs, ours, *tx)
    tx = jnp.stack(tx)
    t_up = lax.ppermute(tx, "ia", y_ring(1))
    t_down = lax.ppermute(tx, "ia", y_ring(-1))

    v2a, v2b, tx = after(v2a, v2b, tx)
    first, rest = FIRST * slab, (cols_j - FIRST) * slab
    theirs0 = product(core, (got, got_core), theirs, (v2a, v2b), 0, first)
    left, theirs0 = after(left, theirs0)
    ours0 = product(flat, (left,), ours, (v2a, v2b), 0, first)
    sent0 = (jnp.concatenate([ours0, theirs0], axis=1) * SCALE).astype(jnp.float16)
    pieces0 = lax.all_to_all(sent0, "vert", 0, 0, tiled=True)

    left, sent0 = after(left, sent0)
    ours1 = product(flat, (left,), ours, (v2a, v2b), first, rest)
    got, ours1 = after(got, ours1)
    theirs1 = product(core, (got, got_core), theirs, (v2a, v2b), first, rest)
    theirs1 = (theirs1 * SCALE).astype(jnp.float16)
    t_up, t_down, theirs1 = after(t_up, t_down, theirs1)
    theirs1 = lax.ppermute(theirs1, "ia", X_HI)
    t_two_a = lax.ppermute(t_up[:2], "ia", y_ring(1))
    t_two_b = lax.ppermute(t_down[2:], "ia", y_ring(-1))
    sent1 = ours1 * SCALE + theirs1.astype(F32)
    sent1_16 = sent1.astype(jnp.float16)
    own1 = lax.dynamic_index_in_dim(sent1, z, 0, keepdims=False)
    own1 -= lax.dynamic_index_in_dim(sent1_16, z, 0, keepdims=False).astype(F32)
    pieces1 = lax.all_to_all(sent1_16, "vert", 0, 0, tiled=True)

    tx, t_down, t_two_a, t_two_b, t_up, sent1_16 = after(tx, t_down, t_two_a, t_two_b, t_up, sent1_16)
    near = order_pieces(y, (tx, t_down, t_two_a, t_two_b, t_up))
    far = lax.ppermute(near, "ja", CORE)

    pieces0, sent1_16, own1, near = after(pieces0, sent1_16, own1, near)
    ladder = ladder_sum(jnp.stack([h, ja // 2, core]), weights, near, far, rows_i)
    sum0 = jnp.sum(pieces0.astype(F32), axis=0)
    size = sum0.shape[0] // 2
    other0 = lax.ppermute(sum0[size:], "ia", X_HI)

    sym_i = lax.dynamic_slice_in_dim(occ_sym, ia * rows_i, rows_i, 0)
    sym_j = lax.dynamic_slice_in_dim(occ_sym, ja * cols_j, cols_j, 0)
    sym_a = lax.dynamic_slice_in_dim(vir_sym, z * rows_a, rows_a, 0)
    sym_ab = jnp.bitwise_xor(sym_a[:, None], vir_sym[None, :]).reshape(rows_a * slab)
    table = jnp.bitwise_xor(sym_j[:, None], sym_ab[None, :])
    pieces1, ladder, other0, table, sym_i = after(pieces1, ladder, other0, table, sym_i)
    sum1 = jnp.sum(pieces1.astype(F32), axis=0)
    return finish(sym_i, (sum0[:size], other0, sum1, own1), ladder, table)


def solution(mesh):
    in_specs = (
        P("ia", "ja", "vert"),
        P("ia", "ja", None),
        P("ia", "vert", None),
        P("ia", "vert", "ja"),
        P(),
        P(),
    )
    out_specs = P("ia", "ja", "vert")
    return jax.shard_map(body, mesh=mesh, in_specs=in_specs, out_specs=out_specs, check_vma=False)
```

```python
import functools

import jax
import jax.numpy as jnp
from jax import lax
from jax.experimental import pallas as pl
from jax.experimental.pallas import tpu as pltpu
from jax.sharding import PartitionSpec as P

F32 = jnp.float32
BF16 = jnp.bfloat16
SCALE = 32.0
FIRST = 6


def cost(us):
    return pl.CostEstimate(flops=int(us * 1e9), bytes_accessed=int(us * 3e6), transcendentals=0)


def swap_blocks(tile):
    turned = tile.T
    top, bottom = turned[:64], turned[64:]
    low = lax.broadcasted_iota(jnp.int32, (64, 128), 1) < 64
    return (
        jnp.where(low, top, pltpu.roll(bottom, 64, 1)),
        jnp.where(low, pltpu.roll(top, 64, 1), bottom),
    )


def turn_body(index, u, out):
    for ip in range(u.shape[0] // 2):
        for kp in range(u.shape[2] // 128):
            lanes = slice(128 * kp, 128 * kp + 128)
            tile = jnp.concatenate([u[2 * ip, :, lanes], u[2 * ip + 1, :, lanes]], axis=0)
            first, second = swap_blocks(tile)
            out[128 * ip : 128 * ip + 64, lanes] = first
            out[128 * ip + 64 : 128 * ip + 128, lanes] = second


def turn_slabs(u, index):
    count, size = index.shape[0], u.shape[0] * 64
    return pl.pallas_call(
        turn_body,
        out_shape=jax.ShapeDtypeStruct((size, count * size), BF16),
        grid_spec=pltpu.PrefetchScalarGridSpec(
            num_scalar_prefetch=1,
            grid=(count,),
            in_specs=[pl.BlockSpec((u.shape[0], 64, size), lambda s, index: (0, 0, index[s]))],
            out_specs=pl.BlockSpec((size, size), lambda s, index: (0, s)),
        ),
        compiler_params=pltpu.CompilerParams(vmem_limit_bytes=60 << 20),
        cost_estimate=cost(0.5 * count),
    )(index.astype(jnp.int32), u)


def near_body(place, near, far, v0, v1, v3, out, left, right):
    size = near.shape[0]

    @pl.when(place[0] == 0)
    def _():
        left[...] = near[:, :size]
        right[:size, :] = v1[...]
        right[size : 2 * size, :] = v3[...]

    @pl.when(place[0] != 0)
    def _():
        left[...] = far[:, :size]
        right[:size, :] = v3[...]
        right[size : 2 * size, :] = v1[...]

    for low, high in ((0, 384), (384, 640)):
        total = jnp.dot(near[low:high, size:], right[:size, :], preferred_element_type=F32)
        total += jnp.dot(far[low:high, size:], right[size:, :], preferred_element_type=F32)
        out[low:high, :] = total + jnp.dot(left[low:high, :], v0[...], preferred_element_type=F32)


def product_near(place, left, parts):
    size, width = parts[0].shape
    side = lambda at: pl.BlockSpec((size, 2 * size), lambda s, place: (0, at))
    whole = lambda x: pl.BlockSpec(x.shape, lambda s, place: (0,) * x.ndim)
    out = jax.ShapeDtypeStruct((size, width), F32)
    return pl.pallas_call(
        near_body,
        out_shape=out,
        grid_spec=pltpu.PrefetchScalarGridSpec(
            num_scalar_prefetch=1,
            grid=(1,),
            in_specs=[side(0), side(2 - len(left))] + [whole(x) for x in parts],
            out_specs=whole(out),
            scratch_shapes=[pltpu.VMEM((size, size), BF16), pltpu.VMEM((2 * size, width), BF16)],
        ),
        compiler_params=pltpu.CompilerParams(vmem_limit_bytes=32 << 20),
        cost_estimate=cost(1),
    )(place.astype(jnp.int32).reshape(1), left[0], left[-1], *parts)


def product_body(start, place, partial_sum, near, far, v2a, v2b, out, left):
    size, width = near.shape[0], out.shape[2]
    columns = slice(start, start + width)

    @pl.when(place[0] == 0)
    def _():
        left[...] = far[...]

    @pl.when(place[0] != 0)
    def _():
        left[...] = near[...]

    right = jnp.concatenate([v2a[:, columns], v2b[:, columns]], axis=0)
    for low, high in ((0, 384), (384, 640)):
        total = partial_sum[low:high, columns]
        total += jnp.dot(left[low:high, :], right, preferred_element_type=F32)
        for at in range(low, high, 128):
            for jp in range(width // 128):
                lanes = slice(128 * jp, 128 * jp + 128)
                tile = total[at - low : at - low + 128, lanes]
                first, second = swap_blocks(tile)
                first, second = tile[:64] - first, tile[64:] - second
                for z in range(8):
                    out[z, at // 8 : at // 8 + 8, lanes] = first[8 * z : 8 * z + 8]
                    out[z, at // 8 + 8 : at // 8 + 16, lanes] = second[8 * z : 8 * z + 8]


def product(place, left, partial_sum, parts, start, width):
    size = partial_sum.shape[0]
    side = lambda at: pl.BlockSpec((size, size), lambda s, place: (0, at))
    whole = lambda x: pl.BlockSpec(x.shape, lambda s, place: (0,) * x.ndim)
    out = jax.ShapeDtypeStruct((8, size // 8, width), F32)
    return pl.pallas_call(
        functools.partial(product_body, start),
        out_shape=out,
        grid_spec=pltpu.PrefetchScalarGridSpec(
            num_scalar_prefetch=1,
            grid=(1,),
            in_specs=[whole(partial_sum), side(0), side(2 * (2 - len(left)))]
            + [whole(x) for x in parts],
            out_specs=whole(out),
            scratch_shapes=[pltpu.VMEM((size, size), BF16)],
        ),
        compiler_params=pltpu.CompilerParams(vmem_limit_bytes=24 << 20),
        cost_estimate=cost(1),
    )(place.astype(jnp.int32).reshape(1), partial_sum, left[0], left[-1], *parts)


def ring(n, shift):
    return [(i, (i + shift) % n) for i in range(n)]


def y_ring(shift):
    return [(4 * h + y, 4 * h + (y + shift) % 4) for h in range(2) for y in range(4)]


X_HI = [(i, (i + 4) % 8) for i in range(8)]
CORE = [(j, j ^ 1) for j in range(4)]
X_LO = [(j, j ^ 2) for j in range(4)]
X_CROSS = [(4 * i + j, 4 * ((i + 4) % 8) + (j ^ 2)) for i in range(8) for j in range(4)]


def after(*values):
    return lax.optimization_barrier(values)


def sort_body(w, order, out, rows):
    count = w.shape[1]
    for i in range(w.shape[0]):
        rows[count * i : count * i + count, :] = w[i].astype(F32)
    out[...] = jnp.dot(rows[...].astype(BF16), order[...], preferred_element_type=F32).astype(BF16)


def sort_columns(weights, order):
    rows_i, cols_j, columns = weights.shape
    rows, width = rows_i * cols_j, order.shape[0]
    return pl.pallas_call(
        sort_body,
        out_shape=jax.ShapeDtypeStruct((rows, columns), BF16),
        grid=(columns // width,),
        in_specs=[
            pl.BlockSpec((rows_i, cols_j, width), lambda s: (0, 0, s)),
            pl.BlockSpec((width, width), lambda s: (0, 0)),
        ],
        out_specs=pl.BlockSpec((rows, width), lambda s: (0, s)),
        scratch_shapes=[pltpu.VMEM((rows, width), F32)],
        compiler_params=pltpu.CompilerParams(vmem_limit_bytes=24 << 20),
        cost_estimate=cost(1),
    )(weights, order)


def arrival_order(occ, cols_j):
    width = 8 * occ
    column = jnp.arange(width)
    block, rest = column // (8 * cols_j), column % (8 * cols_j)
    source = (rest // cols_j) * occ + block * cols_j + rest % cols_j
    return (jnp.arange(width)[:, None] == source[None, :]).astype(BF16)


def order_body(start, own, down, two_a, two_b, up, out):
    count = own.shape[0]
    for n in range(count):
        for d, part in ((0, own), (1, down), (3, up)):
            out[n, lax.rem(start[0] + d, 4)] = part[n]
        two = (two_a, two_b)[n // (count // 2)]
        out[n, lax.rem(start[0] + 2, 4)] = two[n % (count // 2)]


def order_pieces(start, pieces):
    whole = lambda x: pl.BlockSpec(x.shape, lambda s, start: (0,) * x.ndim)
    count, rows, width = pieces[0].shape
    out = jax.ShapeDtypeStruct((count, 4, rows, width), BF16)
    return pl.pallas_call(
        order_body,
        out_shape=out,
        grid_spec=pltpu.PrefetchScalarGridSpec(
            num_scalar_prefetch=1,
            grid=(1,),
            in_specs=[whole(x) for x in pieces],
            out_specs=whole(out),
        ),
        compiler_params=pltpu.CompilerParams(vmem_limit_bytes=16 << 20),
        cost_estimate=cost(0.5),
    )(start.astype(jnp.int32).reshape(1), *pieces).reshape(count, 4 * rows, width)


def ladder_body(place, w, near, far, out, full):
    run = near.shape[1] // 5
    for half in range(2):
        for block in range(4):
            x = (half ^ place[0]) * 2 + ((block // 2) ^ place[1])
            for group in range(5):
                at = (half * 20 + group * 4 + block) * run
                rows = slice(group * run, group * run + run)

                @pl.when(block % 2 == place[2])
                def _():
                    full[at : at + run, :] = near[x, rows, :]

                @pl.when(block % 2 != place[2])
                def _():
                    full[at : at + run, :] = far[x, rows, :]

    rows = out.shape[1]
    total = jnp.dot(w[...], full[...], preferred_element_type=F32)
    for i in range(out.shape[0]):
        out[i] = total[rows * i : rows * i + rows]


def ladder_sum(place, weights, near, far, rows_i):
    whole = lambda x: pl.BlockSpec(x.shape, lambda s, place: (0,) * x.ndim)
    out = jax.ShapeDtypeStruct((rows_i, weights.shape[0] // rows_i, near.shape[2]), F32)
    return pl.pallas_call(
        ladder_body,
        out_shape=out,
        grid_spec=pltpu.PrefetchScalarGridSpec(
            num_scalar_prefetch=1,
            grid=(1,),
            in_specs=[whole(weights), whole(near), whole(far)],
            out_specs=whole(out),
            scratch_shapes=[pltpu.VMEM((weights.shape[1], near.shape[2]), BF16)],
        ),
        compiler_params=pltpu.CompilerParams(vmem_limit_bytes=28 << 20),
        cost_estimate=cost(1),
    )(place.astype(jnp.int32), weights, near, far)


def finish_body(sym_i, sum0, other0, sum1, ladder, table, out, rows):
    low = lax.broadcasted_iota(jnp.int32, (8, 128), 1) < 64
    for i in range(out.shape[0]):
        j = 0
        for part in (sum0, sum1):
            for jp in range(part.shape[1] // 128):
                at = slice(8 * i, 8 * i + 8), slice(128 * jp, 128 * jp + 128)
                tile = part[at] * (1.0 / SCALE)
                if part is sum0:
                    tile += other0[at] * (1.0 / SCALE)
                turned = pltpu.roll(tile, 64, 1)
                even = jnp.where(low, tile, pltpu.roll(turned, 7, 0))
                odd = jnp.where(low, turned, pltpu.roll(tile, 7, 0))
                for ap in range(4):
                    rows[i, ap, j : j + 1, :] = even[2 * ap : 2 * ap + 1]
                    rows[i, ap, j + 1 : j + 2, :] = odd[2 * ap : 2 * ap + 1]
                j += 2
        for ap in range(4):
            lanes = slice(128 * ap, 128 * ap + 128)
            value = rows[i, ap] + ladder[i, :, lanes]
            out[i, :, lanes] = jnp.where(table[:, lanes] == sym_i[i], value, 0.0).astype(BF16)


def finish(sym_i, sums, ladder, table):
    whole = lambda x: pl.BlockSpec(x.shape, lambda s, sym_i: (0,) * x.ndim)
    rows_i, cols_j, width = ladder.shape
    return pl.pallas_call(
        finish_body,
        out_shape=jax.ShapeDtypeStruct(ladder.shape, BF16),
        grid_spec=pltpu.PrefetchScalarGridSpec(
            num_scalar_prefetch=1,
            grid=(1,),
            in_specs=[whole(x) for x in (*sums, ladder, table)],
            out_specs=whole(ladder),
            scratch_shapes=[pltpu.VMEM((rows_i, width // 128, cols_j, 128), F32)],
        ),
        compiler_params=pltpu.CompilerParams(vmem_limit_bytes=56 << 20),
        cost_estimate=cost(1),
    )(sym_i, *sums, ladder, table)


def body(amplitudes, ladder_w, ph_left, ph_right, occ_sym, vir_sym):
    rows_i, local_c = ph_left.shape[:2]
    slab = vir_sym.shape[0]
    occ = occ_sym.shape[0]
    cols_j = ph_right.shape[2] // slab
    rows_a = slab // 8
    ia, ja, z = lax.axis_index("ia"), lax.axis_index("ja"), lax.axis_index("vert")
    h, y, core = ia // 4, ia % 4, ja % 2
    around = (y + jnp.arange(4)) % 4

    right = ph_right.reshape(rows_i * local_c, cols_j * slab)
    half = rows_i * local_c // 2
    up = lax.ppermute(right, "ia", y_ring(1))
    down = lax.ppermute(right, "ia", y_ring(-1))
    t = amplitudes.reshape(rows_i * cols_j, -1)
    tx = [t, lax.ppermute(t, "ja", X_LO), lax.ppermute(t, "ia", X_HI)]
    tx.append(lax.ppermute(t, ("ia", "ja"), X_CROSS))
    mine = turn_slabs(ph_left, (1 - h) * 4 + jnp.roll(around, -2 * core)[:2])
    got = lax.ppermute(mine, ("ia", "ja"), X_CROSS)
    ph_left, mine = after(ph_left, mine)
    left = turn_slabs(ph_left, h * 4 + around)
    w, left, order = after(ladder_w, left, arrival_order(occ, cols_j))
    weights = sort_columns(w, order)

    up, down, weights = after(up, down, weights)
    v2a = lax.ppermute(up[:half], "ia", y_ring(1))
    v2b = lax.ppermute(down[half:], "ia", y_ring(-1))
    flat = jnp.zeros_like(z)
    ours = product_near(flat, (left,), (right, down, up))
    got, ours = after(got, ours)
    got_core = lax.ppermute(got, "ja", CORE)
    theirs = product_near(core, (got, got_core), (right, down, up))

    theirs, ours, *tx = after(theirs, ours, *tx)
    tx = jnp.stack(tx)
    t_up = lax.ppermute(tx, "ia", y_ring(1))
    t_down = lax.ppermute(tx, "ia", y_ring(-1))

    v2a, v2b, tx = after(v2a, v2b, tx)
    first, rest = FIRST * slab, (cols_j - FIRST) * slab
    theirs0 = product(core, (got, got_core), theirs, (v2a, v2b), 0, first)
    left, theirs0 = after(left, theirs0)
    ours0 = product(flat, (left,), ours, (v2a, v2b), 0, first)
    sent0 = (jnp.concatenate([ours0, theirs0], axis=1) * SCALE).astype(jnp.float16)
    pieces0 = lax.all_to_all(sent0, "vert", 0, 0, tiled=True)

    left, sent0 = after(left, sent0)
    ours1 = product(flat, (left,), ours, (v2a, v2b), first, rest)
    got, ours1 = after(got, ours1)
    theirs1 = product(core, (got, got_core), theirs, (v2a, v2b), first, rest)
    theirs1 = (theirs1 * SCALE).astype(jnp.float16)
    t_up, t_down, theirs1 = after(t_up, t_down, theirs1)
    theirs1 = lax.ppermute(theirs1, "ia", X_HI)
    t_two_a = lax.ppermute(t_up[:2], "ia", y_ring(1))
    t_two_b = lax.ppermute(t_down[2:], "ia", y_ring(-1))
    sent1_16 = (ours1 * SCALE + theirs1.astype(F32)).astype(jnp.float16)
    pieces1 = lax.all_to_all(sent1_16, "vert", 0, 0, tiled=True)

    tx, t_down, t_two_a, t_two_b, t_up, sent1_16 = after(tx, t_down, t_two_a, t_two_b, t_up, sent1_16)
    near = order_pieces(y, (tx, t_down, t_two_a, t_two_b, t_up))
    far = lax.ppermute(near, "ja", CORE)

    pieces0, sent1_16, near = after(pieces0, sent1_16, near)
    ladder = ladder_sum(jnp.stack([h, ja // 2, core]), weights, near, far, rows_i)
    sum0 = jnp.sum(pieces0.astype(F32), axis=0)
    size = sum0.shape[0] // 2
    other0 = lax.ppermute(sum0[size:], "ia", X_HI)

    sym_i = lax.dynamic_slice_in_dim(occ_sym, ia * rows_i, rows_i, 0)
    sym_j = lax.dynamic_slice_in_dim(occ_sym, ja * cols_j, cols_j, 0)
    sym_a = lax.dynamic_slice_in_dim(vir_sym, z * rows_a, rows_a, 0)
    sym_ab = jnp.bitwise_xor(sym_a[:, None], vir_sym[None, :]).reshape(rows_a * slab)
    table = jnp.bitwise_xor(sym_j[:, None], sym_ab[None, :])
    pieces1, ladder, other0, table, sym_i = after(pieces1, ladder, other0, table, sym_i)
    sum1 = jnp.sum(pieces1.astype(F32), axis=0)
    return finish(sym_i, (sum0[:size], other0, sum1), ladder, table)


def solution(mesh):
    in_specs = (
        P("ia", "ja", "vert"),
        P("ia", "ja", None),
        P("ia", "vert", None),
        P("ia", "vert", "ja"),
        P(),
        P(),
    )
    out_specs = P("ia", "ja", "vert")
    return jax.shard_map(body, mesh=mesh, in_specs=in_specs, out_specs=out_specs, check_vma=False)
```

```python
import functools

import jax
import jax.numpy as jnp
from jax import lax
from jax.experimental import pallas as pl
from jax.experimental.pallas import tpu as pltpu
from jax.sharding import PartitionSpec as P

F32 = jnp.float32
BF16 = jnp.bfloat16
SCALE = 32.0
FIRST = 6


def cost(us):
    return pl.CostEstimate(flops=int(us * 1e9), bytes_accessed=int(us * 3e6), transcendentals=0)


def swap_blocks(tile):
    turned = tile.T
    top, bottom = turned[:64], turned[64:]
    low = lax.broadcasted_iota(jnp.int32, (64, 128), 1) < 64
    return (
        jnp.where(low, top, pltpu.roll(bottom, 64, 1)),
        jnp.where(low, pltpu.roll(top, 64, 1), bottom),
    )


def turn_body(index, u, out):
    for ip in range(u.shape[0] // 2):
        for kp in range(u.shape[2] // 128):
            lanes = slice(128 * kp, 128 * kp + 128)
            tile = jnp.concatenate([u[2 * ip, :, lanes], u[2 * ip + 1, :, lanes]], axis=0)
            first, second = swap_blocks(tile)
            out[128 * ip : 128 * ip + 64, lanes] = first
            out[128 * ip + 64 : 128 * ip + 128, lanes] = second


def turn_slabs(u, index):
    count, size = index.shape[0], u.shape[0] * 64
    return pl.pallas_call(
        turn_body,
        out_shape=jax.ShapeDtypeStruct((size, count * size), BF16),
        grid_spec=pltpu.PrefetchScalarGridSpec(
            num_scalar_prefetch=1,
            grid=(count,),
            in_specs=[pl.BlockSpec((u.shape[0], 64, size), lambda s, index: (0, 0, index[s]))],
            out_specs=pl.BlockSpec((size, size), lambda s, index: (0, s)),
        ),
        compiler_params=pltpu.CompilerParams(vmem_limit_bytes=60 << 20),
        cost_estimate=cost(0.5 * count),
    )(index.astype(jnp.int32), u)


def near_body(place, near, far, v0, v1, v3, *refs):
    out, left, right = refs[-3:]
    size = near.shape[0]

    @pl.when(place[0] == 0)
    def _():
        left[...] = near[:, :size]
        right[:size, :] = v1[...]
        right[size : 2 * size, :] = v3[...]

    @pl.when(place[0] != 0)
    def _():
        left[...] = far[:, :size]
        right[:size, :] = v3[...]
        right[size : 2 * size, :] = v1[...]

    for low, high in ((0, 384), (384, 640)):
        total = jnp.dot(near[low:high, size:], right[:size, :], preferred_element_type=F32)
        total += jnp.dot(far[low:high, size:], right[size:, :], preferred_element_type=F32)
        out[low:high, :] = total + jnp.dot(left[low:high, :], v0[...], preferred_element_type=F32)


def product_near(place, left, parts, *tokens):
    size, width = parts[0].shape
    side = lambda at: pl.BlockSpec((size, 2 * size), lambda s, place: (0, at))
    whole = lambda x: pl.BlockSpec(x.shape, lambda s, place: (0,) * x.ndim)
    out = jax.ShapeDtypeStruct((size, width), F32)
    return pl.pallas_call(
        near_body,
        out_shape=out,
        grid_spec=pltpu.PrefetchScalarGridSpec(
            num_scalar_prefetch=1,
            grid=(1,),
            in_specs=[side(0), side(2 - len(left))]
            + [whole(x) for x in parts]
            + [pl.BlockSpec(memory_space=pl.ANY)] * len(tokens),
            out_specs=whole(out),
            scratch_shapes=[pltpu.VMEM((size, size), BF16), pltpu.VMEM((2 * size, width), BF16)],
        ),
        compiler_params=pltpu.CompilerParams(vmem_limit_bytes=32 << 20),
        cost_estimate=cost(1),
    )(place.astype(jnp.int32).reshape(1), left[0], left[-1], *parts, *tokens)


def product_body(start, place, partial_sum, near, far, v2a, v2b, out, left):
    size, width = near.shape[0], out.shape[2]
    columns = slice(start, start + width)

    @pl.when(place[0] == 0)
    def _():
        left[...] = far[...]

    @pl.when(place[0] != 0)
    def _():
        left[...] = near[...]

    right = jnp.concatenate([v2a[:, columns], v2b[:, columns]], axis=0)
    for low, high in ((0, 384), (384, 640)):
        total = partial_sum[low:high, columns]
        total += jnp.dot(left[low:high, :], right, preferred_element_type=F32)
        for at in range(low, high, 128):
            for jp in range(width // 128):
                lanes = slice(128 * jp, 128 * jp + 128)
                tile = total[at - low : at - low + 128, lanes]
                first, second = swap_blocks(tile)
                first, second = tile[:64] - first, tile[64:] - second
                for z in range(8):
                    out[z, at // 8 : at // 8 + 8, lanes] = first[8 * z : 8 * z + 8]
                    out[z, at // 8 + 8 : at // 8 + 16, lanes] = second[8 * z : 8 * z + 8]


def product(place, left, partial_sum, parts, start, width):
    size = partial_sum.shape[0]
    side = lambda at: pl.BlockSpec((size, size), lambda s, place: (0, at))
    whole = lambda x: pl.BlockSpec(x.shape, lambda s, place: (0,) * x.ndim)
    out = jax.ShapeDtypeStruct((8, size // 8, width), F32)
    return pl.pallas_call(
        functools.partial(product_body, start),
        out_shape=out,
        grid_spec=pltpu.PrefetchScalarGridSpec(
            num_scalar_prefetch=1,
            grid=(1,),
            in_specs=[whole(partial_sum), side(0), side(2 * (2 - len(left)))]
            + [whole(x) for x in parts],
            out_specs=whole(out),
            scratch_shapes=[pltpu.VMEM((size, size), BF16)],
        ),
        compiler_params=pltpu.CompilerParams(vmem_limit_bytes=24 << 20),
        cost_estimate=cost(1),
    )(place.astype(jnp.int32).reshape(1), partial_sum, left[0], left[-1], *parts)


def ring(n, shift):
    return [(i, (i + shift) % n) for i in range(n)]


def y_ring(shift):
    return [(4 * h + y, 4 * h + (y + shift) % 4) for h in range(2) for y in range(4)]


X_HI = [(i, (i + 4) % 8) for i in range(8)]
CORE = [(j, j ^ 1) for j in range(4)]
X_LO = [(j, j ^ 2) for j in range(4)]
X_CROSS = [(4 * i + j, 4 * ((i + 4) % 8) + (j ^ 2)) for i in range(8) for j in range(4)]


def after(*values):
    return lax.optimization_barrier(values)


def sort_body(w, order, out, rows):
    count = w.shape[1]
    for i in range(w.shape[0]):
        rows[count * i : count * i + count, :] = w[i].astype(F32)
    out[...] = jnp.dot(rows[...].astype(BF16), order[...], preferred_element_type=F32).astype(BF16)


def sort_columns(weights, order):
    rows_i, cols_j, columns = weights.shape
    rows, width = rows_i * cols_j, order.shape[0]
    return pl.pallas_call(
        sort_body,
        out_shape=jax.ShapeDtypeStruct((rows, columns), BF16),
        grid=(columns // width,),
        in_specs=[
            pl.BlockSpec((rows_i, cols_j, width), lambda s: (0, 0, s)),
            pl.BlockSpec((width, width), lambda s: (0, 0)),
        ],
        out_specs=pl.BlockSpec((rows, width), lambda s: (0, s)),
        scratch_shapes=[pltpu.VMEM((rows, width), F32)],
        compiler_params=pltpu.CompilerParams(vmem_limit_bytes=24 << 20),
        cost_estimate=cost(1),
    )(weights, order)


def arrival_order(occ, cols_j):
    width = 8 * occ
    column = jnp.arange(width)
    block, rest = column // (8 * cols_j), column % (8 * cols_j)
    source = (rest // cols_j) * occ + block * cols_j + rest % cols_j
    return (jnp.arange(width)[:, None] == source[None, :]).astype(BF16)


def order_body(start, own, down, two_a, two_b, up, out):
    count = own.shape[0]
    for n in range(count):
        for d, part in ((0, own), (1, down), (3, up)):
            out[n, lax.rem(start[0] + d, 4)] = part[n]
        two = (two_a, two_b)[n // (count // 2)]
        out[n, lax.rem(start[0] + 2, 4)] = two[n % (count // 2)]


def order_pieces(start, pieces):
    whole = lambda x: pl.BlockSpec(x.shape, lambda s, start: (0,) * x.ndim)
    count, rows, width = pieces[0].shape
    out = jax.ShapeDtypeStruct((count, 4, rows, width), BF16)
    return pl.pallas_call(
        order_body,
        out_shape=out,
        grid_spec=pltpu.PrefetchScalarGridSpec(
            num_scalar_prefetch=1,
            grid=(1,),
            in_specs=[whole(x) for x in pieces],
            out_specs=whole(out),
        ),
        compiler_params=pltpu.CompilerParams(vmem_limit_bytes=16 << 20),
        cost_estimate=cost(0.5),
    )(start.astype(jnp.int32).reshape(1), *pieces).reshape(count, 4 * rows, width)


def ladder_body(place, w, near, far, out, full):
    run = near.shape[1] // 5
    for half in range(2):
        for block in range(4):
            x = (half ^ place[0]) * 2 + ((block // 2) ^ place[1])
            for group in range(5):
                at = (half * 20 + group * 4 + block) * run
                rows = slice(group * run, group * run + run)

                @pl.when(block % 2 == place[2])
                def _():
                    full[at : at + run, :] = near[x, rows, :]

                @pl.when(block % 2 != place[2])
                def _():
                    full[at : at + run, :] = far[x, rows, :]

    rows = out.shape[1]
    total = jnp.dot(w[...], full[...], preferred_element_type=F32)
    for i in range(out.shape[0]):
        out[i] = total[rows * i : rows * i + rows]


def ladder_sum(place, weights, near, far, rows_i):
    whole = lambda x: pl.BlockSpec(x.shape, lambda s, place: (0,) * x.ndim)
    out = jax.ShapeDtypeStruct((rows_i, weights.shape[0] // rows_i, near.shape[2]), F32)
    return pl.pallas_call(
        ladder_body,
        out_shape=out,
        grid_spec=pltpu.PrefetchScalarGridSpec(
            num_scalar_prefetch=1,
            grid=(1,),
            in_specs=[whole(weights), whole(near), whole(far)],
            out_specs=whole(out),
            scratch_shapes=[pltpu.VMEM((weights.shape[1], near.shape[2]), BF16)],
        ),
        compiler_params=pltpu.CompilerParams(vmem_limit_bytes=28 << 20),
        cost_estimate=cost(1),
    )(place.astype(jnp.int32), weights, near, far)


def finish_body(sym_i, sum0, other0, sum1, ladder, table, out, rows):
    low = lax.broadcasted_iota(jnp.int32, (8, 128), 1) < 64
    for i in range(out.shape[0]):
        j = 0
        for part in (sum0, sum1):
            for jp in range(part.shape[1] // 128):
                at = slice(8 * i, 8 * i + 8), slice(128 * jp, 128 * jp + 128)
                tile = part[at] * (1.0 / SCALE)
                if part is sum0:
                    tile += other0[at] * (1.0 / SCALE)
                turned = pltpu.roll(tile, 64, 1)
                even = jnp.where(low, tile, pltpu.roll(turned, 7, 0))
                odd = jnp.where(low, turned, pltpu.roll(tile, 7, 0))
                for ap in range(4):
                    rows[i, ap, j : j + 1, :] = even[2 * ap : 2 * ap + 1]
                    rows[i, ap, j + 1 : j + 2, :] = odd[2 * ap : 2 * ap + 1]
                j += 2
        for ap in range(4):
            lanes = slice(128 * ap, 128 * ap + 128)
            value = rows[i, ap] + ladder[i, :, lanes]
            out[i, :, lanes] = jnp.where(table[:, lanes] == sym_i[i], value, 0.0).astype(BF16)


def finish(sym_i, sums, ladder, table):
    whole = lambda x: pl.BlockSpec(x.shape, lambda s, sym_i: (0,) * x.ndim)
    rows_i, cols_j, width = ladder.shape
    return pl.pallas_call(
        finish_body,
        out_shape=jax.ShapeDtypeStruct(ladder.shape, BF16),
        grid_spec=pltpu.PrefetchScalarGridSpec(
            num_scalar_prefetch=1,
            grid=(1,),
            in_specs=[whole(x) for x in (*sums, ladder, table)],
            out_specs=whole(ladder),
            scratch_shapes=[pltpu.VMEM((rows_i, width // 128, cols_j, 128), F32)],
        ),
        compiler_params=pltpu.CompilerParams(vmem_limit_bytes=56 << 20),
        cost_estimate=cost(1),
    )(sym_i, *sums, ladder, table)


def body(amplitudes, ladder_w, ph_left, ph_right, occ_sym, vir_sym):
    rows_i, local_c = ph_left.shape[:2]
    slab = vir_sym.shape[0]
    occ = occ_sym.shape[0]
    cols_j = ph_right.shape[2] // slab
    rows_a = slab // 8
    ia, ja, z = lax.axis_index("ia"), lax.axis_index("ja"), lax.axis_index("vert")
    h, y, core = ia // 4, ia % 4, ja % 2
    around = (y + jnp.arange(4)) % 4

    right = ph_right.reshape(rows_i * local_c, cols_j * slab)
    half = rows_i * local_c // 2
    up = lax.ppermute(right, "ia", y_ring(1))
    down = lax.ppermute(right, "ia", y_ring(-1))
    t = amplitudes.reshape(rows_i * cols_j, -1)
    tx = [t, lax.ppermute(t, "ja", X_LO), lax.ppermute(t, "ia", X_HI)]
    tx.append(lax.ppermute(t, ("ia", "ja"), X_CROSS))
    mine = turn_slabs(ph_left, (1 - h) * 4 + jnp.roll(around, -2 * core)[:2])
    got = lax.ppermute(mine, ("ia", "ja"), X_CROSS)
    ph_left, mine = after(ph_left, mine)
    left = turn_slabs(ph_left, h * 4 + around)
    w, left, order = after(ladder_w, left, arrival_order(occ, cols_j))
    weights = sort_columns(w, order)

    up, down, weights = after(up, down, weights)
    v2a = lax.ppermute(up[:half], "ia", y_ring(1))
    v2b = lax.ppermute(down[half:], "ia", y_ring(-1))
    flat = jnp.zeros_like(z)
    ours = product_near(flat, (left,), (right, down, up), tx[1])
    got, ours = after(got, ours)
    got_core = lax.ppermute(got, "ja", CORE)
    theirs = product_near(core, (got, got_core), (right, down, up))

    theirs, ours, *tx = after(theirs, ours, *tx)
    tx = jnp.stack(tx)
    t_up = lax.ppermute(tx, "ia", y_ring(1))
    t_down = lax.ppermute(tx, "ia", y_ring(-1))

    v2a, v2b, tx = after(v2a, v2b, tx)
    first, rest = FIRST * slab, (cols_j - FIRST) * slab
    theirs0 = product(core, (got, got_core), theirs, (v2a, v2b), 0, first)
    left, theirs0 = after(left, theirs0)
    ours0 = product(flat, (left,), ours, (v2a, v2b), 0, first)
    sent0 = (jnp.concatenate([ours0, theirs0], axis=1) * SCALE).astype(jnp.float16)
    pieces0 = lax.all_to_all(sent0, "vert", 0, 0, tiled=True)

    left, sent0 = after(left, sent0)
    ours1 = product(flat, (left,), ours, (v2a, v2b), first, rest)
    got, ours1 = after(got, ours1)
    theirs1 = product(core, (got, got_core), theirs, (v2a, v2b), first, rest)
    theirs1 = (theirs1 * SCALE).astype(jnp.float16)
    t_up, t_down, theirs1 = after(t_up, t_down, theirs1)
    theirs1 = lax.ppermute(theirs1, "ia", X_HI)
    t_two_a = lax.ppermute(t_up[:2], "ia", y_ring(1))
    t_two_b = lax.ppermute(t_down[2:], "ia", y_ring(-1))
    sent1_16 = (ours1 * SCALE + theirs1.astype(F32)).astype(jnp.float16)
    pieces1 = lax.all_to_all(sent1_16, "vert", 0, 0, tiled=True)

    tx, t_down, t_two_a, t_two_b, t_up, sent1_16 = after(tx, t_down, t_two_a, t_two_b, t_up, sent1_16)
    near = order_pieces(y, (tx, t_down, t_two_a, t_two_b, t_up))
    far = lax.ppermute(near, "ja", CORE)

    pieces0, sent1_16, near = after(pieces0, sent1_16, near)
    ladder = ladder_sum(jnp.stack([h, ja // 2, core]), weights, near, far, rows_i)
    sum0 = jnp.sum(pieces0.astype(F32), axis=0)
    size = sum0.shape[0] // 2
    other0 = lax.ppermute(sum0[size:], "ia", X_HI)

    sym_i = lax.dynamic_slice_in_dim(occ_sym, ia * rows_i, rows_i, 0)
    sym_j = lax.dynamic_slice_in_dim(occ_sym, ja * cols_j, cols_j, 0)
    sym_a = lax.dynamic_slice_in_dim(vir_sym, z * rows_a, rows_a, 0)
    sym_ab = jnp.bitwise_xor(sym_a[:, None], vir_sym[None, :]).reshape(rows_a * slab)
    table = jnp.bitwise_xor(sym_j[:, None], sym_ab[None, :])
    pieces1, ladder, other0, table, sym_i = after(pieces1, ladder, other0, table, sym_i)
    sum1 = jnp.sum(pieces1.astype(F32), axis=0)
    return finish(sym_i, (sum0[:size], other0, sum1), ladder, table)


def solution(mesh):
    in_specs = (
        P("ia", "ja", "vert"),
        P("ia", "ja", None),
        P("ia", "vert", None),
        P("ia", "vert", "ja"),
        P(),
        P(),
    )
    out_specs = P("ia", "ja", "vert")
    return jax.shard_map(body, mesh=mesh, in_specs=in_specs, out_specs=out_specs, check_vma=False)
```

```python
import functools

import jax
import jax.numpy as jnp
from jax import lax
from jax.experimental import pallas as pl
from jax.experimental.pallas import tpu as pltpu
from jax.sharding import PartitionSpec as P

F32 = jnp.float32
BF16 = jnp.bfloat16
SCALE = 32.0
FIRST = 6


def cost(us):
    return pl.CostEstimate(flops=int(us * 1e9), bytes_accessed=int(us * 3e6), transcendentals=0)


def swap_blocks(tile):
    turned = tile.T
    top, bottom = turned[:64], turned[64:]
    low = lax.broadcasted_iota(jnp.int32, (64, 128), 1) < 64
    return (
        jnp.where(low, top, pltpu.roll(bottom, 64, 1)),
        jnp.where(low, pltpu.roll(top, 64, 1), bottom),
    )


def turn_body(index, u, out):
    for ip in range(u.shape[0] // 2):
        for kp in range(u.shape[2] // 128):
            lanes = slice(128 * kp, 128 * kp + 128)
            tile = jnp.concatenate([u[2 * ip, :, lanes], u[2 * ip + 1, :, lanes]], axis=0)
            first, second = swap_blocks(tile)
            out[128 * ip : 128 * ip + 64, lanes] = first
            out[128 * ip + 64 : 128 * ip + 128, lanes] = second


def turn_slabs(u, index):
    count, size = index.shape[0], u.shape[0] * 64
    return pl.pallas_call(
        turn_body,
        out_shape=jax.ShapeDtypeStruct((size, count * size), BF16),
        grid_spec=pltpu.PrefetchScalarGridSpec(
            num_scalar_prefetch=1,
            grid=(count,),
            in_specs=[pl.BlockSpec((u.shape[0], 64, size), lambda s, index: (0, 0, index[s]))],
            out_specs=pl.BlockSpec((size, size), lambda s, index: (0, s)),
        ),
        compiler_params=pltpu.CompilerParams(vmem_limit_bytes=60 << 20),
        cost_estimate=cost(0.5 * count),
    )(index.astype(jnp.int32), u)


def near_body(place, near, far, v0, v1, v3, *refs):
    out, left, right = refs[-3:]
    size = near.shape[0]

    @pl.when(place[0] == 0)
    def _():
        left[...] = near[:, :size]
        right[:size, :] = v1[...]
        right[size : 2 * size, :] = v3[...]

    @pl.when(place[0] != 0)
    def _():
        left[...] = far[:, :size]
        right[:size, :] = v3[...]
        right[size : 2 * size, :] = v1[...]

    for low, high in ((0, 384), (384, 640)):
        total = jnp.dot(near[low:high, size:], right[:size, :], preferred_element_type=F32)
        total += jnp.dot(far[low:high, size:], right[size:, :], preferred_element_type=F32)
        out[low:high, :] = total + jnp.dot(left[low:high, :], v0[...], preferred_element_type=F32)


def product_near(place, left, parts, *tokens):
    size, width = parts[0].shape
    side = lambda at: pl.BlockSpec((size, 2 * size), lambda s, place: (0, at))
    whole = lambda x: pl.BlockSpec(x.shape, lambda s, place: (0,) * x.ndim)
    out = jax.ShapeDtypeStruct((size, width), F32)
    return pl.pallas_call(
        near_body,
        out_shape=out,
        grid_spec=pltpu.PrefetchScalarGridSpec(
            num_scalar_prefetch=1,
            grid=(1,),
            in_specs=[side(0), side(2 - len(left))]
            + [whole(x) for x in parts]
            + [pl.BlockSpec(memory_space=pl.ANY)] * len(tokens),
            out_specs=whole(out),
            scratch_shapes=[pltpu.VMEM((size, size), BF16), pltpu.VMEM((2 * size, width), BF16)],
        ),
        compiler_params=pltpu.CompilerParams(vmem_limit_bytes=32 << 20),
        cost_estimate=cost(1),
    )(place.astype(jnp.int32).reshape(1), left[0], left[-1], *parts, *tokens)


def product_body(start, place, partial_sum, near, far, v2a, v2b, out, left):
    size, width = near.shape[0], out.shape[2]
    columns = slice(start, start + width)

    @pl.when(place[0] == 0)
    def _():
        left[...] = far[...]

    @pl.when(place[0] != 0)
    def _():
        left[...] = near[...]

    right = jnp.concatenate([v2a[:, columns], v2b[:, columns]], axis=0)
    for low, high in ((0, 384), (384, 640)):
        total = partial_sum[low:high, columns]
        total += jnp.dot(left[low:high, :], right, preferred_element_type=F32)
        for at in range(low, high, 128):
            for jp in range(width // 128):
                lanes = slice(128 * jp, 128 * jp + 128)
                tile = total[at - low : at - low + 128, lanes]
                first, second = swap_blocks(tile)
                first, second = tile[:64] - first, tile[64:] - second
                for z in range(8):
                    out[z, at // 8 : at // 8 + 8, lanes] = first[8 * z : 8 * z + 8]
                    out[z, at // 8 + 8 : at // 8 + 16, lanes] = second[8 * z : 8 * z + 8]


def product(place, left, partial_sum, parts, start, width):
    size = partial_sum.shape[0]
    side = lambda at: pl.BlockSpec((size, size), lambda s, place: (0, at))
    whole = lambda x: pl.BlockSpec(x.shape, lambda s, place: (0,) * x.ndim)
    out = jax.ShapeDtypeStruct((8, size // 8, width), F32)
    return pl.pallas_call(
        functools.partial(product_body, start),
        out_shape=out,
        grid_spec=pltpu.PrefetchScalarGridSpec(
            num_scalar_prefetch=1,
            grid=(1,),
            in_specs=[whole(partial_sum), side(0), side(2 * (2 - len(left)))]
            + [whole(x) for x in parts],
            out_specs=whole(out),
            scratch_shapes=[pltpu.VMEM((size, size), BF16)],
        ),
        compiler_params=pltpu.CompilerParams(vmem_limit_bytes=24 << 20),
        cost_estimate=cost(1),
    )(place.astype(jnp.int32).reshape(1), partial_sum, left[0], left[-1], *parts)


def ring(n, shift):
    return [(i, (i + shift) % n) for i in range(n)]


def y_ring(shift):
    return [(4 * h + y, 4 * h + (y + shift) % 4) for h in range(2) for y in range(4)]


X_HI = [(i, (i + 4) % 8) for i in range(8)]
CORE = [(j, j ^ 1) for j in range(4)]
X_LO = [(j, j ^ 2) for j in range(4)]
X_CROSS = [(4 * i + j, 4 * ((i + 4) % 8) + (j ^ 2)) for i in range(8) for j in range(4)]


def after(*values):
    return lax.optimization_barrier(values)


def sort_body(w, order, out, rows):
    count = w.shape[1]
    for i in range(w.shape[0]):
        rows[count * i : count * i + count, :] = w[i].astype(F32)
    out[...] = jnp.dot(rows[...].astype(BF16), order[...], preferred_element_type=F32).astype(BF16)


def sort_columns(weights, order):
    rows_i, cols_j, columns = weights.shape
    rows, width = rows_i * cols_j, order.shape[0]
    return pl.pallas_call(
        sort_body,
        out_shape=jax.ShapeDtypeStruct((rows, columns), BF16),
        grid=(columns // width,),
        in_specs=[
            pl.BlockSpec((rows_i, cols_j, width), lambda s: (0, 0, s)),
            pl.BlockSpec((width, width), lambda s: (0, 0)),
        ],
        out_specs=pl.BlockSpec((rows, width), lambda s: (0, s)),
        scratch_shapes=[pltpu.VMEM((rows, width), F32)],
        compiler_params=pltpu.CompilerParams(vmem_limit_bytes=24 << 20),
        cost_estimate=cost(1),
    )(weights, order)


def arrival_order(occ, cols_j):
    width = 8 * occ
    column = jnp.arange(width)
    block, rest = column // (8 * cols_j), column % (8 * cols_j)
    source = (rest // cols_j) * occ + block * cols_j + rest % cols_j
    return (jnp.arange(width)[:, None] == source[None, :]).astype(BF16)


def order_body(start, own, down, two_a, two_b, up, out):
    count = own.shape[0]
    for n in range(count):
        for d, part in ((0, own), (1, down), (3, up)):
            out[n, lax.rem(start[0] + d, 4)] = part[n]
        two = (two_a, two_b)[n // (count // 2)]
        out[n, lax.rem(start[0] + 2, 4)] = two[n % (count // 2)]


def order_pieces(start, pieces):
    whole = lambda x: pl.BlockSpec(x.shape, lambda s, start: (0,) * x.ndim)
    count, rows, width = pieces[0].shape
    out = jax.ShapeDtypeStruct((count, 4, rows, width), BF16)
    return pl.pallas_call(
        order_body,
        out_shape=out,
        grid_spec=pltpu.PrefetchScalarGridSpec(
            num_scalar_prefetch=1,
            grid=(1,),
            in_specs=[whole(x) for x in pieces],
            out_specs=whole(out),
        ),
        compiler_params=pltpu.CompilerParams(vmem_limit_bytes=16 << 20),
        cost_estimate=cost(0.5),
    )(start.astype(jnp.int32).reshape(1), *pieces).reshape(count, 4 * rows, width)


def ladder_body(place, w, near, far, out, full):
    run = near.shape[1] // 5
    for half in range(2):
        for block in range(4):
            x = (half ^ place[0]) * 2 + ((block // 2) ^ place[1])
            for group in range(5):
                at = (half * 20 + group * 4 + block) * run
                rows = slice(group * run, group * run + run)

                @pl.when(block % 2 == place[2])
                def _():
                    full[at : at + run, :] = near[x, rows, :]

                @pl.when(block % 2 != place[2])
                def _():
                    full[at : at + run, :] = far[x, rows, :]

    rows = out.shape[1]
    total = jnp.dot(w[...], full[...], preferred_element_type=F32)
    for i in range(out.shape[0]):
        out[i] = total[rows * i : rows * i + rows]


def ladder_sum(place, weights, near, far, rows_i):
    whole = lambda x: pl.BlockSpec(x.shape, lambda s, place: (0,) * x.ndim)
    out = jax.ShapeDtypeStruct((rows_i, weights.shape[0] // rows_i, near.shape[2]), F32)
    return pl.pallas_call(
        ladder_body,
        out_shape=out,
        grid_spec=pltpu.PrefetchScalarGridSpec(
            num_scalar_prefetch=1,
            grid=(1,),
            in_specs=[whole(weights), whole(near), whole(far)],
            out_specs=whole(out),
            scratch_shapes=[pltpu.VMEM((weights.shape[1], near.shape[2]), BF16)],
        ),
        compiler_params=pltpu.CompilerParams(vmem_limit_bytes=28 << 20),
        cost_estimate=cost(1),
    )(place.astype(jnp.int32), weights, near, far)


def finish_body(sym_i, sum0, other0, sum1, ladder, table, out, rows):
    low = lax.broadcasted_iota(jnp.int32, (8, 128), 1) < 64
    for i in range(out.shape[0]):
        j = 0
        for part in (sum0, sum1):
            for jp in range(part.shape[1] // 128):
                at = slice(8 * i, 8 * i + 8), slice(128 * jp, 128 * jp + 128)
                tile = part[at] * (1.0 / SCALE)
                if part is sum0:
                    tile += other0[at] * (1.0 / SCALE)
                turned = pltpu.roll(tile, 64, 1)
                even = jnp.where(low, tile, pltpu.roll(turned, 7, 0))
                odd = jnp.where(low, turned, pltpu.roll(tile, 7, 0))
                for ap in range(4):
                    rows[i, ap, j : j + 1, :] = even[2 * ap : 2 * ap + 1]
                    rows[i, ap, j + 1 : j + 2, :] = odd[2 * ap : 2 * ap + 1]
                j += 2
        for ap in range(4):
            lanes = slice(128 * ap, 128 * ap + 128)
            value = rows[i, ap] + ladder[i, :, lanes]
            out[i, :, lanes] = jnp.where(table[:, lanes] == sym_i[i], value, 0.0).astype(BF16)


def finish(sym_i, sums, ladder, table):
    whole = lambda x: pl.BlockSpec(x.shape, lambda s, sym_i: (0,) * x.ndim)
    rows_i, cols_j, width = ladder.shape
    return pl.pallas_call(
        finish_body,
        out_shape=jax.ShapeDtypeStruct(ladder.shape, BF16),
        grid_spec=pltpu.PrefetchScalarGridSpec(
            num_scalar_prefetch=1,
            grid=(1,),
            in_specs=[whole(x) for x in (*sums, ladder, table)],
            out_specs=whole(ladder),
            scratch_shapes=[pltpu.VMEM((rows_i, width // 128, cols_j, 128), F32)],
        ),
        compiler_params=pltpu.CompilerParams(vmem_limit_bytes=56 << 20),
        cost_estimate=cost(1),
    )(sym_i, *sums, ladder, table)


def body(amplitudes, ladder_w, ph_left, ph_right, occ_sym, vir_sym):
    rows_i, local_c = ph_left.shape[:2]
    slab = vir_sym.shape[0]
    occ = occ_sym.shape[0]
    cols_j = ph_right.shape[2] // slab
    rows_a = slab // 8
    ia, ja, z = lax.axis_index("ia"), lax.axis_index("ja"), lax.axis_index("vert")
    h, y, core = ia // 4, ia % 4, ja % 2
    around = (y + jnp.arange(4)) % 4

    right = ph_right.reshape(rows_i * local_c, cols_j * slab)
    half = rows_i * local_c // 2
    up = lax.ppermute(right, "ia", y_ring(1))
    down = lax.ppermute(right, "ia", y_ring(-1))
    t = amplitudes.reshape(rows_i * cols_j, -1)
    tx = [t, lax.ppermute(t, "ja", X_LO), lax.ppermute(t, "ia", X_HI)]
    tx.append(lax.ppermute(t, ("ia", "ja"), X_CROSS))
    mine = turn_slabs(ph_left, (1 - h) * 4 + jnp.roll(around, -2 * core)[:2])
    got = lax.ppermute(mine, ("ia", "ja"), X_CROSS)
    ph_left, mine = after(ph_left, mine)
    left = turn_slabs(ph_left, h * 4 + around)
    w, left, order = after(ladder_w, left, arrival_order(occ, cols_j))
    weights = sort_columns(w, order)

    up, down, weights = after(up, down, weights)
    v2a = lax.ppermute(up[:half], "ia", y_ring(1))
    v2b = lax.ppermute(down[half:], "ia", y_ring(-1))
    flat = jnp.zeros_like(z)
    ours = product_near(flat, (left,), (right, down, up), tx[1], got)
    got, ours = after(got, ours)
    got_core = lax.ppermute(got, "ja", CORE)
    theirs = product_near(core, (got, got_core), (right, down, up))

    theirs, ours, *tx = after(theirs, ours, *tx)
    tx = jnp.stack(tx)
    t_up = lax.ppermute(tx, "ia", y_ring(1))
    t_down = lax.ppermute(tx, "ia", y_ring(-1))

    v2a, v2b, tx = after(v2a, v2b, tx)
    first, rest = FIRST * slab, (cols_j - FIRST) * slab
    theirs0 = product(core, (got, got_core), theirs, (v2a, v2b), 0, first)
    left, theirs0 = after(left, theirs0)
    ours0 = product(flat, (left,), ours, (v2a, v2b), 0, first)
    sent0 = (jnp.concatenate([ours0, theirs0], axis=1) * SCALE).astype(jnp.float16)
    pieces0 = lax.all_to_all(sent0, "vert", 0, 0, tiled=True)

    left, sent0 = after(left, sent0)
    ours1 = product(flat, (left,), ours, (v2a, v2b), first, rest)
    got, ours1 = after(got, ours1)
    theirs1 = product(core, (got, got_core), theirs, (v2a, v2b), first, rest)
    theirs1 = (theirs1 * SCALE).astype(jnp.float16)
    t_up, t_down, theirs1 = after(t_up, t_down, theirs1)
    theirs1 = lax.ppermute(theirs1, "ia", X_HI)
    t_two_a = lax.ppermute(t_up[:2], "ia", y_ring(1))
    t_two_b = lax.ppermute(t_down[2:], "ia", y_ring(-1))
    sent1_16 = (ours1 * SCALE + theirs1.astype(F32)).astype(jnp.float16)
    pieces1 = lax.all_to_all(sent1_16, "vert", 0, 0, tiled=True)

    tx, t_down, t_two_a, t_two_b, t_up, sent1_16 = after(tx, t_down, t_two_a, t_two_b, t_up, sent1_16)
    near = order_pieces(y, (tx, t_down, t_two_a, t_two_b, t_up))
    far = lax.ppermute(near, "ja", CORE)

    pieces0, sent1_16, near = after(pieces0, sent1_16, near)
    ladder = ladder_sum(jnp.stack([h, ja // 2, core]), weights, near, far, rows_i)
    sum0 = jnp.sum(pieces0.astype(F32), axis=0)
    size = sum0.shape[0] // 2
    other0 = lax.ppermute(sum0[size:], "ia", X_HI)

    sym_i = lax.dynamic_slice_in_dim(occ_sym, ia * rows_i, rows_i, 0)
    sym_j = lax.dynamic_slice_in_dim(occ_sym, ja * cols_j, cols_j, 0)
    sym_a = lax.dynamic_slice_in_dim(vir_sym, z * rows_a, rows_a, 0)
    sym_ab = jnp.bitwise_xor(sym_a[:, None], vir_sym[None, :]).reshape(rows_a * slab)
    table = jnp.bitwise_xor(sym_j[:, None], sym_ab[None, :])
    pieces1, ladder, other0, table, sym_i = after(pieces1, ladder, other0, table, sym_i)
    sum1 = jnp.sum(pieces1.astype(F32), axis=0)
    return finish(sym_i, (sum0[:size], other0, sum1), ladder, table)


def solution(mesh):
    in_specs = (
        P("ia", "ja", "vert"),
        P("ia", "ja", None),
        P("ia", "vert", None),
        P("ia", "vert", "ja"),
        P(),
        P(),
    )
    out_specs = P("ia", "ja", "vert")
    return jax.shard_map(body, mesh=mesh, in_specs=in_specs, out_specs=out_specs, check_vma=False)
```
